512 devices in a mesh: row: 64 (over y, x, core), col: 8 (over z).
Axes of the slice: x: 4, y: 8, z: 8, core: 2. Of those that a mesh axis runs over, the one named last changes fastest.
Arguments:
- matrix: bfloat16 [4, 16384, 1, 2048], P(None, 'row', None, 'col'), may hold values from -0.045 to 2.375, as said below
Outputs:
- factored: float32 [4, 16384, 1, 2048], P(None, 'row', None, 'col')
The draws below stay inside these ranges and needn't reach their ends.
Inputs may be any that keep to these rules, and one draw needn't show every extreme that they name: Only entries on or below the diagonal are read. The symmetric matrix built from the lower triangle has its leading 2 * 256 principal block positive definite.
All inputs are finite; a program needn't handle non-finite values.
Results may differ from the reference program's by a relative error of at most 0.0003.
Values sent between devices are 32-bit elements; how exact they have to be, the bound alone decides.
A program may use at most 64 MiB of HBM per device.

```python
import jax
import jax.numpy as jnp
from jax import lax

NB = 256
RB_DEV = 4
CB_DEV = 1
N = 65536
CW = 2048


def draw_matrix(key, part):
    key = jax.random.fold_in(key, 11)
    key_off, key_diag = jax.random.split(key)
    offdiag = jax.random.uniform(key_off, (N, CW), jnp.float32, -0.045, 0.045)
    diagonal = jax.random.uniform(key_diag, (N, CW), jnp.float32, 1.6, 2.375)
    rows_ids = jnp.arange(N, dtype=jnp.int32)[:, None]
    cols_ids = jnp.arange(CW, dtype=jnp.int32)[None, :]
    values = jnp.where(rows_ids == cols_ids, diagonal, offdiag)
    return values.astype(jnp.bfloat16).reshape(RB_DEV, N // RB_DEV, CB_DEV, CW // CB_DEV)


def setup_inputs(seed: int = 0) -> dict:
    key_of = jax.random.split(jax.random.key(seed), 2)
    return {
        "matrix": draw_matrix(jax.random.fold_in(key_of[1], 71), 0),
    }


def reference(matrix):
    high = lax.Precision.HIGHEST
    window = matrix.astype(jnp.float32).reshape(N, CW)
    block_ids = (jnp.arange(N, dtype=jnp.int32) // NB)[:, None]
    for section in range(2):
        start = section * NB
        diag_block = window[start:start + NB, start:start + NB]
        symmetric = jnp.tril(diag_block) + jnp.tril(diag_block, -1).T
        lower = jnp.linalg.cholesky(symmetric)
        inverse = jax.scipy.linalg.solve_triangular(lower, jnp.eye(NB, dtype=jnp.float32), lower=True)
        panel = jnp.dot(window[:, start:start + NB], inverse.T, precision=high)
        column = jnp.where(block_ids > section, panel, jnp.float32(0.0))
        column = column.at[start:start + NB].set(lower)
        update = jnp.dot(column, column[start + NB:CW].T, precision=high)
        window = window.at[:, start + NB:].add(-update)
        window = window.at[:, start:start + NB].set(column)
    rows_ids = jnp.arange(N, dtype=jnp.int32)[:, None]
    cols_ids = jnp.arange(CW, dtype=jnp.int32)[None, :]
    window = jnp.where(rows_ids >= cols_ids, window, jnp.float32(0.0))
    return window.reshape(RB_DEV, N // RB_DEV, CB_DEV, CW // CB_DEV)
```

```python
import jax
import jax.numpy as jnp
from jax import lax
from jax.experimental import pallas as pl
from jax.experimental.pallas import tpu as pltpu
from jax.sharding import PartitionSpec as P

MESH = pl.DeviceIdType.MESH
F32 = jnp.float32
NB = 256
STEP = 32
XS, YS, ZS = 4, 8, 8
R = 32
SKEW = 3
PER = 128 // R
CHUNKS = 4 * PER
PIECE = NB // YS
INV0, P10, INV1, AJ0, AJ1 = range(5)


def split3(x):
    h = x.astype(jnp.bfloat16)
    r = x - h.astype(F32)
    m = r.astype(jnp.bfloat16)
    return h, m, (r - m.astype(F32)).astype(jnp.bfloat16)


def mm_nt(a, b):
    return lax.dot_general(a, b, (((1,), (1,)), ((), ())), precision=lax.Precision.HIGHEST, preferred_element_type=F32)


def mm_nn(a, b):
    return lax.dot_general(a, b, (((1,), (0,)), ((), ())), precision=lax.Precision.HIGHEST, preferred_element_type=F32)


def iota(shape, d):
    return lax.broadcasted_iota(jnp.int32, shape, d)


def symmetric(x):
    keep = iota((NB, NB), 0) >= iota((NB, NB), 1)
    return jnp.where(keep, x, x.T)


def factor_start(W, a):
    W[:, 0:NB] = a
    W[:, NB:2 * NB] = jnp.where(iota((NB, NB), 0) == iota((NB, NB), 1), 1.0, 0.0).astype(F32)


def factor_step(W, k):
    base = pl.multiple_of(STEP * k, STEP)
    ra = W[pl.ds(base, STEP), 0:NB]
    rm = W[pl.ds(base, STEP), NB:2 * NB]
    ra = pltpu.roll(ra, lax.rem(NB - STEP * k, NB), 1)
    G = [[ra[8 * g:8 * g + 8, 0:128], ra[8 * g:8 * g + 8, 128:256],
          rm[8 * g:8 * g + 8, 0:128], rm[8 * g:8 * g + 8, 128:256]] for g in range(4)]
    full = (8, 128)
    sub = iota(full, 0)
    for t in range(4):
        cols = {g: [jnp.broadcast_to(G[g][0][:, 8 * t + i:8 * t + i + 1], full) for i in range(8)] for g in range(t, 4)}
        s = {(i, j): jnp.broadcast_to(cols[t][j][i:i + 1, :], full) for j in range(8) for i in range(j, 8)}
        row = [[jnp.broadcast_to(G[t][v][i:i + 1, :], full) for v in range(4)] for i in range(8)]
        for j in range(8):
            r = lax.rsqrt(s[j, j])
            for i in range(j + 1, 8):
                s[i, j] = s[i, j] * r
            for i2 in range(j + 1, 8):
                for i in range(i2, 8):
                    s[i, i2] = s[i, i2] - s[i, j] * s[i2, j]
            row[j] = [x * r for x in row[j]]
            for i in range(j + 1, 8):
                row[i] = [x - s[i, j] * y for x, y in zip(row[i], row[j])]
            for g in range(t + 1, 4):
                cols[g][j] = cols[g][j] * r
                for i in range(j + 1, 8):
                    cols[g][i] = cols[g][i] - s[i, j] * cols[g][j]
        for g in range(t + 1, 4):
            for v in range(4):
                p = [cols[g][j] * row[j][v] for j in range(8)]
                while len(p) > 1:
                    p = [a + b for a, b in zip(p[::2], p[1::2])]
                G[g][v] = G[g][v] - p[0]
        for v in range(4):
            x = row[0][v]
            for i in range(1, 8):
                x = jnp.where(sub == i, row[i][v], x)
            G[t][v] = x
    ua = jnp.concatenate([jnp.concatenate([G[g][0], G[g][1]], 1) for g in range(4)], 0)
    um = jnp.concatenate([jnp.concatenate([G[g][2], G[g][3]], 1) for g in range(4)], 0)
    ua = pltpu.roll(ua, STEP * k, 1)
    lhs = jnp.where(iota((STEP, NB), 1) >= STEP * (k + 1), ua, 0.0)
    W[pl.ds(base, STEP), 0:NB] = ua
    W[pl.ds(base, STEP), NB:2 * NB] = um
    a, b, c = split3(lhs)
    ah, am, al = split3(ua)
    mh, mm, ml = split3(um)
    left = jnp.concatenate([a, a, b, a, c, b], 0)
    dn = (((0,), (0,)), ((), ()))
    for lo, (h, m, l) in ((0, (ah, am, al)), (NB, (mh, mm, ml))):
        right = jnp.concatenate([h, m, h, l, h, m], 0)
        W[:, lo:lo + NB] = W[:, lo:lo + NB] - lax.dot_general(left, right, dn, preferred_element_type=F32)


def kernel(a_ref, o_ref, x0, x1, D, E, W, zsend, zrecv, bsend, brecv, ssend, srecv, esend, erecv):
    row = lax.axis_index("row")
    z = lax.axis_index("col")
    core = lax.rem(row, 2)
    x = lax.rem(row // 2, XS)
    y = row // (2 * XS)

    def at(x_, y_, z_, c_):
        return ((y_ * XS + x_) * 2 + c_, z_)

    is_src = (row == 0) & (z == 0)
    is_a11 = (row == 1) & (z == 1)
    is_a10 = (row == 1) & (z == 0)

    barrier = pltpu.get_barrier_semaphore()
    for d in range(1, ZS):
        pl.semaphore_signal(barrier, inc=1, device_id=at(x, y, lax.rem(z + d, ZS), core), device_id_type=MESH)
    for d in range(1, YS):
        pl.semaphore_signal(barrier, inc=1, device_id=at(x, lax.rem(y + d, YS), z, core), device_id_type=MESH)
    for d in range(1, XS):
        pl.semaphore_signal(barrier, inc=1, device_id=at(lax.rem(x + d, XS), y, z, core), device_id_type=MESH)
    pl.semaphore_signal(barrier, inc=1, device_id=at(x, y, z, 1 - core), device_id_type=MESH)

    @pl.when(is_src)
    def _():
        pl.semaphore_signal(barrier, inc=1, device_id=(1, 1), device_id_type=MESH)

    @pl.when(is_a11)
    def _():
        pl.semaphore_signal(barrier, inc=1, device_id=(0, 0), device_id_type=MESH)

    @pl.when(z == 0)
    def _():
        for s in range(4):
            x0[s] = a_ref[s].astype(F32)

        @pl.when(row == 0)
        def _():
            x0[0] = symmetric(x0[0])

    @pl.when(z == 1)
    def _():
        for s in range(4):
            x1[s] = a_ref[s].astype(F32)

        @pl.when(row == 1)
        def _():
            x1[0] = symmetric(x1[0])

    @pl.when(is_src)
    def _():
        factor_start(W, x0[0])

    pl.semaphore_wait(barrier, ZS + YS + XS - 2 + jnp.where(is_src | is_a11, 1, 0))

    def send_a10():
        return pltpu.make_async_remote_copy(src_ref=x0.at[0], dst_ref=E.at[0], send_sem=esend.at[0], recv_sem=erecv.at[0],
                                            device_id=(0, 0), device_id_type=MESH)

    def send_a11():
        return pltpu.make_async_remote_copy(src_ref=x1.at[0], dst_ref=E.at[1], send_sem=esend.at[0], recv_sem=erecv.at[1],
                                            device_id=(0, 0), device_id_type=MESH)

    @pl.when(is_a10)
    def _():
        send_a10().start()

    @pl.when(is_a11)
    def _():
        send_a11().start()

    zp = lax.rem(z + 1, ZS)
    zm = lax.rem(z + ZS - 1, ZS)
    hops = (z, lax.rem(ZS - z, ZS), lax.rem(z + ZS - 1, ZS), lax.rem(ZS + 1 - z, ZS))
    last = (ZS - 1, 1, ZS - 1, 2)

    def zcopy(st, c):
        buf = x0 if st < 2 else x1
        off = pl.multiple_of((0 if st % 2 == 0 else 128) + lax.rem(c, PER) * R, R)
        ref = buf.at[c // PER, pl.ds(off, R), :]
        return pltpu.make_async_remote_copy(src_ref=ref, dst_ref=ref, send_sem=zsend.at[st, c], recv_sem=zrecv.at[st, c],
                                            device_id=(row, zp if st % 2 == 0 else zm), device_id_type=MESH)

    def zreceives(st):
        return (hops[st] > 0) & (z != 0) if st == 2 else hops[st] > 0

    def zsends(st):
        return (z != last[st]) & (z != 0) if st == 2 else z != last[st]

    def ztick(n):
        for st in range(4):
            c = n - hops[st] * SKEW
            ok = (c >= 0) & (c < CHUNKS)

            @pl.when(ok & zreceives(st))
            def _():
                zcopy(st, c).wait_recv()

            @pl.when(ok & zsends(st))
            def _():
                zcopy(st, c).start()

    def root(b):
        if b < AJ0:
            return 0, 0, 0
        return z // 2, z, lax.rem(z, 2)

    def has(b):
        return z >= (0 if b == INV0 else 1 if b < AJ0 else 2)

    def piece(b, q, dest, sem):
        ref = D.at[b, pl.ds(pl.multiple_of(q * PIECE, PIECE), PIECE), :]
        return pltpu.make_async_remote_copy(src_ref=ref, dst_ref=ref, send_sem=bsend.at[b, sem], recv_sem=brecv.at[b, q],
                                            device_id=dest, device_id_type=MESH)

    def on_root(b):
        xr, zr, cr = root(b)
        return (x == xr) & (y == 0) & (z == zr) & (core == cr)

    def scatter(b, act):
        for d in range(1, YS):
            act(piece(b, d, at(x, d, z, core), d - 1))

    def send_x(b, act):
        for d in range(1, XS):
            act(piece(b, y, at(lax.rem(x + d, XS), y, z, core), 6 + d))

    def send_z(b, act):
        for d in range(1, ZS):
            act(piece(b, y, at(x, y, d, core), 9 + d))

    def send_y(b, act):
        xr, zr, _ = root(b)
        for d in range(1, YS):
            to = lax.rem(y + d, YS)

            @pl.when(jnp.logical_not((to == 0) & (x == xr) & (z == zr)))
            def _():
                act(piece(b, y, at(x, to, z, core), 16 + d))

    def start(cp):
        cp.start()

    def finish(cp):
        cp.wait_send()

    def relay_roles(b):
        xr, zr, cr = root(b)
        on_core = core == cr
        first = on_core & (x == xr) & (z == zr)
        second = on_core & (z == zr) if b < AJ0 else None
        third = on_core & has(b)
        return first, second, third

    def relay_sends(b, act):
        first, second, third = relay_roles(b)

        @pl.when(first & (z >= (2 if b >= AJ0 else 0)))
        def _():
            send_x(b, act)

        if second is not None:
            @pl.when(second)
            def _():
                send_z(b, act)

        @pl.when(third)
        def _():
            send_y(b, act)

    def relay(b):
        xr, zr, cr = root(b)
        takes = (core == cr) & (has(b) | (z == zr)) if b < AJ0 else (core == cr) & has(b)

        @pl.when(takes & jnp.logical_not(on_root(b)))
        def _():
            piece(b, y, at(x, y, z, 1 - core), 0).wait_recv()

        relay_sends(b, start)

    def sibling(b):
        return pltpu.make_async_remote_copy(src_ref=D.at[b], dst_ref=D.at[b], send_sem=ssend.at[b], recv_sem=srecv.at[b],
                                            device_id=at(x, y, z, 1 - core), device_id_type=MESH)

    def collect(b):
        cr = root(b)[2]

        @pl.when((core == cr) & has(b))
        def _():
            @pl.when(jnp.logical_not(on_root(b)))
            def _():
                for d in range(1, YS):
                    piece(b, lax.rem(y + d, YS), at(x, y, z, 1 - core), 0).wait_recv()
            sibling(b).start()

        @pl.when((core != cr) & has(b))
        def _():
            sibling(b).wait_recv()

    def drain(b):
        cr = root(b)[2]

        @pl.when(on_root(b) & (z >= (2 if b >= AJ0 else 0)))
        def _():
            scatter(b, finish)

        relay_sends(b, finish)

        @pl.when((core == cr) & has(b))
        def _():
            sibling(b).wait_send()

    def factor_tick(n):
        @pl.when(is_src)
        def _():
            @pl.when(n < 8)
            def _():
                factor_step(W, n)

            @pl.when(n == 8)
            def _():
                inv0 = W[:, NB:2 * NB]
                D[INV0] = inv0
                scatter(INV0, start)
                send_a10().wait_recv()
                send_a11().wait_recv()
                p10 = mm_nt(E[0], inv0)
                D[P10] = p10
                scatter(P10, start)
                factor_start(W, E[1] - mm_nt(p10, p10))

            @pl.when((n > 8) & (n < 17))
            def _():
                factor_step(W, n - 9)

            @pl.when(n == 17)
            def _():
                D[INV1] = W[:, NB:2 * NB]
                scatter(INV1, start)

    def tick(n, carry):
        ztick(n)
        factor_tick(n)
        return carry

    lax.fori_loop(0, CHUNKS + (ZS - 1) * SKEW, tick, 0)

    @pl.when(on_root(AJ0) & (z >= 2))
    def _():
        D[AJ0] = x0[0]
        D[AJ1] = x1[0]
        scatter(AJ0, start)
        scatter(AJ1, start)

    order = (INV0, P10, AJ0, AJ1, INV1)
    for b in order:
        relay(b)
    for b in order:
        collect(b)

    @pl.when(z == 0)
    def _():
        E[0] = D[INV0]

    @pl.when(z >= 1)
    def _():
        inv0, p10, inv1 = D[INV0], D[P10], D[INV1]

        @pl.when(z == 1)
        def _():
            E[1] = inv1
            E[0] = mm_nn(-mm_nn(inv1, p10), inv0)

        @pl.when(z >= 2)
        def _():
            pj0 = mm_nt(D[AJ0], inv0)
            pj1 = mm_nt(D[AJ1] - mm_nt(pj0, p10), inv1)
            t1 = -mm_nn(pj1, inv1)
            E[1] = t1
            E[0] = -mm_nn(pj0 + mm_nn(t1, p10), inv0)

    dn = (((1,), (1,)), ((), ()))
    for s in range(4):
        acc = jnp.where(z >= 2, a_ref[s].astype(F32), 0.0)
        xs = x0[s].astype(jnp.bfloat16)
        for t in split3(E[0])[::-1]:
            acc = acc + lax.dot_general(xs, t, dn, preferred_element_type=F32)
        o_ref[s] = acc

        @pl.when(z >= 1)
        def _():
            acc = o_ref[s]
            xs = x1[s].astype(jnp.bfloat16)
            for t in split3(E[1])[::-1]:
                acc = acc + lax.dot_general(xs, t, dn, preferred_element_type=F32)
            o_ref[s] = acc

    @pl.when(row <= z)
    def _():
        keep = row * NB + iota((NB, NB), 0) >= z * NB + iota((NB, NB), 1)
        o_ref[0] = jnp.where(keep, o_ref[0], 0.0)

    @pl.when(is_a10)
    def _():
        send_a10().wait_send()

    @pl.when(is_a11)
    def _():
        send_a11().wait_send()

    def zdrain(c, carry):
        for st in range(4):
            @pl.when(zsends(st))
            def _():
                zcopy(st, c).wait_send()
        return carry

    lax.fori_loop(0, CHUNKS, zdrain, 0)
    for b in order:
        drain(b)


def per_device(matrix):
    a = matrix.reshape(4, NB, NB)
    dma = pltpu.SemaphoreType.DMA
    out = pl.pallas_call(
        kernel,
        out_shape=jax.ShapeDtypeStruct((4, NB, NB), F32),
        in_specs=[pl.BlockSpec(memory_space=pltpu.VMEM)],
        out_specs=pl.BlockSpec(memory_space=pltpu.VMEM),
        scratch_shapes=[
            pltpu.VMEM((4, NB, NB), F32),
            pltpu.VMEM((4, NB, NB), F32),
            pltpu.VMEM((5, NB, NB), F32),
            pltpu.VMEM((2, NB, NB), F32),
            pltpu.VMEM((NB, 2 * NB), F32),
            dma((4, CHUNKS)), dma((4, CHUNKS)),
            dma((5, 24)), dma((5, YS)),
            dma((5,)), dma((5,)),
            dma((1,)), dma((2,)),
        ],
        compiler_params=pltpu.CompilerParams(collective_id=0, has_side_effects=True, vmem_limit_bytes=40 << 20),
    )(a)
    return out.reshape(4, NB, 1, NB)


def solution(mesh):
    return jax.shard_map(
        per_device,
        mesh=mesh,
        in_specs=(P(None, "row", None, "col"),),
        out_specs=P(None, "row", None, "col"),
        check_vma=False,
    )
```

```python
import jax
import jax.numpy as jnp
from jax import lax
from jax.experimental import pallas as pl
from jax.experimental.pallas import tpu as pltpu
from jax.sharding import PartitionSpec as P

MESH = pl.DeviceIdType.MESH
F32 = jnp.float32
NB = 256
STEP = 32
XS, YS, ZS = 4, 8, 8
R = 32
SKEW = 12
UNITS = 4 * NB // R
RING = 13
COUNT = UNITS - RING
EARLY = 4
MID = 4
TICKS = 40
PIECE = NB // YS
INV0, P10, INV1, AJ0, AJ1 = range(5)
AT_INV0, AT_P10, AT_INV1, AT_AJ = 3, 9, 11, 6
TO_X, TO_Z = 3, 4


def split3(x):
    h = x.astype(jnp.bfloat16)
    r = x - h.astype(F32)
    m = r.astype(jnp.bfloat16)
    return h, m, (r - m.astype(F32)).astype(jnp.bfloat16)


def mm_nt(a, b):
    return lax.dot_general(a, b, (((1,), (1,)), ((), ())), precision=lax.Precision.HIGHEST, preferred_element_type=F32)


def mm_nn(a, b):
    return lax.dot_general(a, b, (((1,), (0,)), ((), ())), precision=lax.Precision.HIGHEST, preferred_element_type=F32)


def iota(shape, d):
    return lax.broadcasted_iota(jnp.int32, shape, d)


def symmetric(x):
    keep = iota((NB, NB), 0) >= iota((NB, NB), 1)
    return jnp.where(keep, x, x.T)


def factor_start(W, a):
    W[:, 0:NB] = a
    W[:, NB:2 * NB] = jnp.where(iota((NB, NB), 0) == iota((NB, NB), 1), 1.0, 0.0).astype(F32)


def factor_step(W, k):
    base = pl.multiple_of(STEP * k, STEP)
    ra = W[pl.ds(base, STEP), 0:NB]
    rm = W[pl.ds(base, STEP), NB:2 * NB]
    ra = pltpu.roll(ra, lax.rem(NB - STEP * k, NB), 1)
    G = [[ra[8 * g:8 * g + 8, 0:128], ra[8 * g:8 * g + 8, 128:256],
          rm[8 * g:8 * g + 8, 0:128], rm[8 * g:8 * g + 8, 128:256]] for g in range(4)]
    full = (8, 128)
    sub = iota(full, 0)
    for t in range(4):
        cols = {g: [jnp.broadcast_to(G[g][0][:, 8 * t + i:8 * t + i + 1], full) for i in range(8)] for g in range(t, 4)}
        s = {(i, j): jnp.broadcast_to(cols[t][j][i:i + 1, :], full) for j in range(8) for i in range(j, 8)}
        row = [[jnp.broadcast_to(G[t][v][i:i + 1, :], full) for v in range(4)] for i in range(8)]
        for j in range(8):
            r = lax.rsqrt(s[j, j])
            for i in range(j + 1, 8):
                s[i, j] = s[i, j] * r
            for i2 in range(j + 1, 8):
                for i in range(i2, 8):
                    s[i, i2] = s[i, i2] - s[i, j] * s[i2, j]
            row[j] = [x * r for x in row[j]]
            for i in range(j + 1, 8):
                row[i] = [x - s[i, j] * y for x, y in zip(row[i], row[j])]
            for g in range(t + 1, 4):
                cols[g][j] = cols[g][j] * r
                for i in range(j + 1, 8):
                    cols[g][i] = cols[g][i] - s[i, j] * cols[g][j]
        for g in range(t + 1, 4):
            for v in range(4):
                p = [cols[g][j] * row[j][v] for j in range(8)]
                while len(p) > 1:
                    p = [a + b for a, b in zip(p[::2], p[1::2])]
                G[g][v] = G[g][v] - p[0]
        for v in range(4):
            x = row[0][v]
            for i in range(1, 8):
                x = jnp.where(sub == i, row[i][v], x)
            G[t][v] = x
    ua = jnp.concatenate([jnp.concatenate([G[g][0], G[g][1]], 1) for g in range(4)], 0)
    um = jnp.concatenate([jnp.concatenate([G[g][2], G[g][3]], 1) for g in range(4)], 0)
    ua = pltpu.roll(ua, STEP * k, 1)
    lhs = jnp.where(iota((STEP, NB), 1) >= STEP * (k + 1), ua, 0.0)
    W[pl.ds(base, STEP), 0:NB] = ua
    W[pl.ds(base, STEP), NB:2 * NB] = um
    a, b, c = split3(lhs)
    ah, am, al = split3(ua)
    mh, mm, ml = split3(um)
    left = jnp.concatenate([a, a, b, a, c, b], 0)
    dn = (((0,), (0,)), ((), ()))
    for lo, (h, m, l) in ((0, (ah, am, al)), (NB, (mh, mm, ml))):
        right = jnp.concatenate([h, m, h, l, h, m], 0)
        W[:, lo:lo + NB] = W[:, lo:lo + NB] - lax.dot_general(left, right, dn, preferred_element_type=F32)


def kernel(m_ref, o_ref, a_ref, x0, x1, D, E, W, asem, zsend, zrecv, bsend, brecv, ssend, srecv, esend, erecv):
    row = lax.axis_index("row")
    z = lax.axis_index("col")
    core = lax.rem(row, 2)
    x = lax.rem(row // 2, XS)
    y = row // (2 * XS)

    def at(x_, y_, z_, c_):
        return ((y_ * XS + x_) * 2 + c_, z_)

    is_src = (row == 0) & (z == 0)
    is_a11 = (row == 1) & (z == 1)
    is_a10 = (row == 1) & (z == 0)

    barrier = pltpu.get_barrier_semaphore()
    for d in range(1, ZS):
        pl.semaphore_signal(barrier, inc=1, device_id=at(x, y, lax.rem(z + d, ZS), core), device_id_type=MESH)
    for d in range(1, YS):
        pl.semaphore_signal(barrier, inc=1, device_id=at(x, lax.rem(y + d, YS), z, core), device_id_type=MESH)
    for d in range(1, XS):
        pl.semaphore_signal(barrier, inc=1, device_id=at(lax.rem(x + d, XS), y, z, core), device_id_type=MESH)
    pl.semaphore_signal(barrier, inc=1, device_id=at(x, y, z, 1 - core), device_id_type=MESH)

    @pl.when(is_src)
    def _():
        pl.semaphore_signal(barrier, inc=1, device_id=(1, 1), device_id_type=MESH)

    @pl.when(is_a11)
    def _():
        pl.semaphore_signal(barrier, inc=1, device_id=(0, 0), device_id_type=MESH)

    hands = (row >= 2) & (row < ZS) & (z < 2)
    line = (z >= 2) & (x == z // 2) & (core == lax.rem(z, 2)) & (y > 0)

    @pl.when(hands)
    def _():
        for q in range(1, YS):
            pl.semaphore_signal(barrier, inc=1, device_id=at(x, q, row, core), device_id_type=MESH)

    @pl.when(line)
    def _():
        for p in range(2):
            pl.semaphore_signal(barrier, inc=1, device_id=(z, p), device_id_type=MESH)

    own = pltpu.make_async_copy(m_ref, a_ref, asem)
    own.start()
    own.wait()

    @pl.when(z == 0)
    def _():
        for s in range(4):
            x0[s] = a_ref[s].astype(F32)

        @pl.when(row == 0)
        def _():
            x0[0] = symmetric(x0[0])

    @pl.when(z == 1)
    def _():
        for s in range(4):
            x1[s] = a_ref[s].astype(F32)

        @pl.when(row == 1)
        def _():
            x1[0] = symmetric(x1[0])

    @pl.when(is_src)
    def _():
        factor_start(W, x0[0])

        def step(k, carry):
            factor_step(W, k)
            return carry

        lax.fori_loop(0, EARLY, step, 0)

    peers = ZS + YS + XS - 2 + jnp.where(is_src | is_a11, 1, 0)
    pl.semaphore_wait(barrier, peers + jnp.where(hands, YS - 1, 0) + jnp.where(line, 2, 0))

    def send_a10():
        return pltpu.make_async_remote_copy(src_ref=x0.at[0], dst_ref=E.at[0], send_sem=esend.at[0], recv_sem=erecv.at[0],
                                            device_id=(0, 0), device_id_type=MESH)

    def send_a11():
        return pltpu.make_async_remote_copy(src_ref=x1.at[0], dst_ref=E.at[1], send_sem=esend.at[0], recv_sem=erecv.at[1],
                                            device_id=(0, 0), device_id_type=MESH)

    @pl.when(is_a10)
    def _():
        send_a10().start()

    @pl.when(is_a11)
    def _():
        send_a11().start()

    def hand(p, q):
        rows = pl.ds(q * PIECE, PIECE)
        return pltpu.make_async_remote_copy(src_ref=(x0, x1)[p].at[0, rows, :], dst_ref=D.at[AJ0 + p, rows, :],
                                            send_sem=bsend.at[AJ0 + p, q], recv_sem=brecv.at[AJ0 + p, q],
                                            device_id=at(x, q, row, core), device_id_type=MESH)

    def hand_all(act):
        for p in range(2):
            @pl.when(hands & (z == p))
            def _():
                for q in range(YS):
                    act(hand(p, q))

    hand_all(lambda cp: cp.start())

    hops = z, lax.rem(ZS - z, ZS), lax.rem(z + ZS - 1, ZS), lax.rem(ZS + 1 - z, ZS), z
    up, down = lax.rem(z + 1, ZS), lax.rem(z + ZS - 1, ZS)

    def zcopy(st, c):
        buf = x0 if st < 2 or st == 4 else x1
        odd = 0 if st in (0, 2) else 1
        u = jnp.where(c < RING, 2 * c + odd, c + RING)
        per = NB // R
        ref = buf.at[u // per, pl.ds(pl.multiple_of(lax.rem(u, per) * R, R), R), :]
        return pltpu.make_async_remote_copy(src_ref=ref, dst_ref=ref, send_sem=zsend.at[st, c], recv_sem=zrecv.at[st, c],
                                            device_id=(row, down if st in (1, 3) else up), device_id_type=MESH)

    def takes(st, c):
        if st == 0:
            return (z >= 1) & ((c < RING) | (z <= MID))
        if st == 1:
            return (z >= 2) & ((c < RING) | (z > MID))
        if st == 2:
            return (z >= 2) & ((c < RING) | (z <= MID))
        if st == 3:
            return (z != 1) & ((c < RING) | (z == 0) | (z > MID))
        return (z == 1) & (c < RING)

    def passes(st, c):
        if st == 0:
            return (z < ZS - 1) & ((c < RING) | (z < MID))
        if st == 1:
            return (z != 1) & (z != 2) & ((c < RING) | (z == 0) | (z > MID + 1))
        if st == 2:
            return (z >= 1) & (z < ZS - 1) & ((c < RING) | (z < MID))
        if st == 3:
            return (z != 2) & ((c < RING) | (z < 2) | (z > MID + 1))
        return (z == 0) & (c < RING)

    def ztick(n):
        for st in range(5):
            c = n - (hops[st] * SKEW) // 4
            ok = (c >= 0) & (c < COUNT)

            @pl.when(ok & takes(st, c))
            def _():
                zcopy(st, c).wait_recv()

            if st in (0, 1, 4):
                @pl.when(ok & passes(st, c) & jnp.logical_not(is_src))
                def _():
                    zcopy(st, c).start()

                for c in (2 * n, 2 * n + 1):
                    @pl.when(is_src & (c < COUNT) & passes(st, c))
                    def _():
                        zcopy(st, c).start()
            else:
                @pl.when(ok & passes(st, c))
                def _():
                    zcopy(st, c).start()

    def root(b):
        if b < AJ0:
            return 0, 0, 0
        return z // 2, z, lax.rem(z, 2)

    def has(b):
        return z >= (0 if b == INV0 else 1 if b < AJ0 else 2)

    def piece(b, q, dest, sem):
        ref = D.at[b, pl.ds(pl.multiple_of(q * PIECE, PIECE), PIECE), :]
        return pltpu.make_async_remote_copy(src_ref=ref, dst_ref=ref, send_sem=bsend.at[b, sem], recv_sem=brecv.at[b, q],
                                            device_id=dest, device_id_type=MESH)

    def on_root(b):
        xr, zr, cr = root(b)
        return (x == xr) & (y == 0) & (z == zr) & (core == cr) & (b < AJ0)

    def scatter(b, act):
        for d in range(1, YS):
            act(piece(b, d, at(x, d, z, core), d - 1))

    def send_x(b, act):
        for d in range(1, XS):
            act(piece(b, y, at(lax.rem(x + d, XS), y, z, core), 7 + d))

    def send_z(b, act):
        for d in range(1, ZS):
            act(piece(b, y, at(x, y, d, core), 10 + d))

    def send_y(b, act):
        xr, zr, _ = root(b)
        for d in range(1, YS):
            to = lax.rem(y + d, YS)

            @pl.when(jnp.logical_not((to == 0) & (x == xr) & (z == zr) & (b < AJ0)))
            def _():
                act(piece(b, y, at(x, to, z, core), 17 + d))

    def start(cp):
        cp.start()

    def finish(cp):
        cp.wait_send()

    def relay_sends(b, act):
        xr, zr, cr = root(b)
        on_core = core == cr

        @pl.when(on_core & (x == xr) & (z == zr) & (z >= (2 if b >= AJ0 else 0)))
        def _():
            send_x(b, act)

        if b < AJ0:
            @pl.when(on_core & (z == zr))
            def _():
                send_z(b, act)

        @pl.when(on_core & has(b))
        def _():
            send_y(b, act)

    def relay(b):
        xr, zr, cr = root(b)
        gets = (core == cr) & ((has(b) | (z == zr)) if b < AJ0 else has(b))

        @pl.when(gets & jnp.logical_not(on_root(b)))
        def _():
            piece(b, y, at(x, y, z, 1 - core), 0).wait_recv()
            relay_sends(b, start)

    def sibling(b):
        return pltpu.make_async_remote_copy(src_ref=D.at[b], dst_ref=D.at[b], send_sem=ssend.at[b], recv_sem=srecv.at[b],
                                            device_id=at(x, y, z, 1 - core), device_id_type=MESH)

    def collect(b):
        cr = root(b)[2]

        @pl.when((core == cr) & has(b))
        def _():
            @pl.when(jnp.logical_not(on_root(b)))
            def _():
                for d in range(1, YS):
                    piece(b, lax.rem(y + d, YS), at(x, y, z, 1 - core), 0).wait_recv()
            sibling(b).start()

        @pl.when((core != cr) & has(b))
        def _():
            sibling(b).wait_recv()

    def drain(b):
        cr = root(b)[2]

        @pl.when(on_root(b))
        def _():
            scatter(b, finish)

        relay_sends(b, finish)

        @pl.when((core == cr) & has(b))
        def _():
            sibling(b).wait_send()

    def stream(b, k):
        rows = pl.ds(pl.multiple_of(k * PIECE, PIECE), PIECE)
        D[b, rows, :] = W[rows, NB:2 * NB]

        @pl.when(k > 0)
        def _():
            piece(b, k, at(x, k, z, core), k - 1).start()

        @pl.when(k == 0)
        def _():
            relay_sends(b, start)

    def factor_tick(n):
        k = n + EARLY
        at_p10 = NB // STEP

        @pl.when(is_src & (k < at_p10))
        def _():
            factor_step(W, k)
            stream(INV0, k)

        @pl.when(is_src & (k == at_p10))
        def _():
            send_a10().wait_recv()
            send_a11().wait_recv()
            p10 = mm_nt(E[0], D[INV0])
            D[P10] = p10
            scatter(P10, start)
            relay_sends(P10, start)
            factor_start(W, E[1] - mm_nt(p10, p10))

        @pl.when(is_src & (k > at_p10) & (k <= at_p10 + NB // STEP))
        def _():
            factor_step(W, k - at_p10 - 1)
            stream(INV1, k - at_p10 - 1)

    @pl.when(is_src)
    def _():
        def early(k, carry):
            stream(INV0, k)
            return carry

        lax.fori_loop(0, EARLY, early, 0)

    order = (INV0, P10, AJ0, AJ1, INV1)

    def relay_at(b):
        xr, zr, _ = root(b)
        t = {INV0: AT_INV0 + jnp.maximum(y + 1 - EARLY, 0), P10: AT_P10, INV1: AT_INV1 + y, AJ0: AT_AJ, AJ1: AT_AJ}[b]
        return t + jnp.where(x == xr, 0, TO_X) + (jnp.where(z == zr, 0, TO_Z) if b < AJ0 else 0)

    when = [relay_at(b) for b in order]

    def tick(n, carry):
        ztick(n)
        factor_tick(n)

        for b, t in zip(order, when):
            @pl.when(n == t)
            def _():
                relay(b)
        return carry

    lax.fori_loop(0, TICKS, tick, 0)

    for b in order:
        collect(b)

    @pl.when(z == 0)
    def _():
        E[0] = D[INV0]

    @pl.when(z >= 1)
    def _():
        inv0, p10, inv1 = D[INV0], D[P10], D[INV1]

        @pl.when(z == 1)
        def _():
            E[1] = inv1
            E[0] = mm_nn(-mm_nn(inv1, p10), inv0)

        @pl.when(z >= 2)
        def _():
            pj0 = mm_nt(D[AJ0], inv0)
            pj1 = mm_nt(D[AJ1] - mm_nt(pj0, p10), inv1)
            t1 = -mm_nn(pj1, inv1)
            E[1] = t1
            E[0] = -mm_nn(pj0 + mm_nn(t1, p10), inv0)

    dn = (((1,), (1,)), ((), ()))
    for s in range(4):
        acc = jnp.where(z >= 2, a_ref[s].astype(F32), 0.0)
        xs = x0[s].astype(jnp.bfloat16)
        for t in split3(E[0])[::-1]:
            acc = acc + lax.dot_general(xs, t, dn, preferred_element_type=F32)
        o_ref[s] = acc

        @pl.when(z >= 1)
        def _():
            acc = o_ref[s]
            xs = x1[s].astype(jnp.bfloat16)
            for t in split3(E[1])[::-1]:
                acc = acc + lax.dot_general(xs, t, dn, preferred_element_type=F32)
            o_ref[s] = acc

    @pl.when(row <= z)
    def _():
        keep = row * NB + iota((NB, NB), 0) >= z * NB + iota((NB, NB), 1)
        o_ref[0] = jnp.where(keep, o_ref[0], 0.0)

    @pl.when(is_a10)
    def _():
        send_a10().wait_send()

    @pl.when(is_a11)
    def _():
        send_a11().wait_send()

    def zdrain(c, carry):
        for st in range(5):
            @pl.when(passes(st, c))
            def _():
                zcopy(st, c).wait_send()
        return carry

    lax.fori_loop(0, COUNT, zdrain, 0)

    hand_all(finish)
    for b in order:
        drain(b)


def per_device(matrix):
    a = matrix.reshape(4, NB, NB)
    dma = pltpu.SemaphoreType.DMA
    out = pl.pallas_call(
        kernel,
        out_shape=jax.ShapeDtypeStruct((4, NB, NB), F32),
        in_specs=[pl.BlockSpec(memory_space=pl.ANY)],
        out_specs=pl.BlockSpec(memory_space=pltpu.VMEM),
        scratch_shapes=[
            pltpu.VMEM((4, NB, NB), jnp.bfloat16),
            pltpu.VMEM((4, NB, NB), F32),
            pltpu.VMEM((4, NB, NB), F32),
            pltpu.VMEM((5, NB, NB), F32),
            pltpu.VMEM((2, NB, NB), F32),
            pltpu.VMEM((NB, 2 * NB), F32),
            dma(()), dma((5, COUNT)), dma((5, COUNT)),
            dma((5, 25)), dma((5, YS)),
            dma((5,)), dma((5,)),
            dma((1,)), dma((2,)),
        ],
        compiler_params=pltpu.CompilerParams(collective_id=0, has_side_effects=True, vmem_limit_bytes=40 << 20),
    )(a)
    return out.reshape(4, NB, 1, NB)


def solution(mesh):
    return jax.shard_map(
        per_device,
        mesh=mesh,
        in_specs=(P(None, "row", None, "col"),),
        out_specs=P(None, "row", None, "col"),
        check_vma=False,
    )
```

```python
import jax
import jax.numpy as jnp
from jax import lax
from jax.experimental import pallas as pl
from jax.experimental.pallas import tpu as pltpu
from jax.sharding import PartitionSpec as P

MESH = pl.DeviceIdType.MESH
F32 = jnp.float32
NB = 256
STEP = 32
XS, YS, ZS = 4, 8, 8
R = 32
SKEW = 12
UNITS = 4 * NB // R
RING = 13
COUNT = UNITS - RING
EARLY = 4
MID = 4
TICKS = 40
PIECE = NB // YS
INV0, P10, INV1, AJ0, AJ1 = range(5)
AT_INV0, AT_P10, AT_INV1, AT_AJ, AT_HAND = 3, 9, 11, 9, 4
TO_X, TO_Z = 3, 4


def split3(x):
    h = x.astype(jnp.bfloat16)
    r = x - h.astype(F32)
    m = r.astype(jnp.bfloat16)
    return h, m, (r - m.astype(F32)).astype(jnp.bfloat16)


def mm_nt(a, b):
    return lax.dot_general(a, b, (((1,), (1,)), ((), ())), precision=lax.Precision.HIGHEST, preferred_element_type=F32)


def mm_nn(a, b):
    return lax.dot_general(a, b, (((1,), (0,)), ((), ())), precision=lax.Precision.HIGHEST, preferred_element_type=F32)


def iota(shape, d):
    return lax.broadcasted_iota(jnp.int32, shape, d)


def symmetric(x):
    keep = iota((NB, NB), 0) >= iota((NB, NB), 1)
    return jnp.where(keep, x, x.T)


def factor_start(W, a):
    W[:, 0:NB] = a
    W[:, NB:2 * NB] = jnp.where(iota((NB, NB), 0) == iota((NB, NB), 1), 1.0, 0.0).astype(F32)


def factor_step(W, k):
    base = pl.multiple_of(STEP * k, STEP)
    ra = W[pl.ds(base, STEP), 0:NB]
    rm = W[pl.ds(base, STEP), NB:2 * NB]
    ra = pltpu.roll(ra, lax.rem(NB - STEP * k, NB), 1)
    G = [[ra[8 * g:8 * g + 8, 0:128], ra[8 * g:8 * g + 8, 128:256],
          rm[8 * g:8 * g + 8, 0:128], rm[8 * g:8 * g + 8, 128:256]] for g in range(4)]
    full = (8, 128)
    sub = iota(full, 0)
    for t in range(4):
        cols = {g: [jnp.broadcast_to(G[g][0][:, 8 * t + i:8 * t + i + 1], full) for i in range(8)] for g in range(t, 4)}
        s = {(i, j): jnp.broadcast_to(cols[t][j][i:i + 1, :], full) for j in range(8) for i in range(j, 8)}
        row = [[jnp.broadcast_to(G[t][v][i:i + 1, :], full) for v in range(4)] for i in range(8)]
        for j in range(8):
            r = lax.rsqrt(s[j, j])
            for i in range(j + 1, 8):
                s[i, j] = s[i, j] * r
            for i2 in range(j + 1, 8):
                for i in range(i2, 8):
                    s[i, i2] = s[i, i2] - s[i, j] * s[i2, j]
            row[j] = [x * r for x in row[j]]
            for i in range(j + 1, 8):
                row[i] = [x - s[i, j] * y for x, y in zip(row[i], row[j])]
            for g in range(t + 1, 4):
                cols[g][j] = cols[g][j] * r
                for i in range(j + 1, 8):
                    cols[g][i] = cols[g][i] - s[i, j] * cols[g][j]
        for g in range(t + 1, 4):
            for v in range(4):
                p = [cols[g][j] * row[j][v] for j in range(8)]
                while len(p) > 1:
                    p = [a + b for a, b in zip(p[::2], p[1::2])]
                G[g][v] = G[g][v] - p[0]
        for v in range(4):
            x = row[0][v]
            for i in range(1, 8):
                x = jnp.where(sub == i, row[i][v], x)
            G[t][v] = x
    ua = jnp.concatenate([jnp.concatenate([G[g][0], G[g][1]], 1) for g in range(4)], 0)
    um = jnp.concatenate([jnp.concatenate([G[g][2], G[g][3]], 1) for g in range(4)], 0)
    ua = pltpu.roll(ua, STEP * k, 1)
    lhs = jnp.where(iota((STEP, NB), 1) >= STEP * (k + 1), ua, 0.0)
    W[pl.ds(base, STEP), 0:NB] = ua
    W[pl.ds(base, STEP), NB:2 * NB] = um
    a, b, c = split3(lhs)
    ah, am, al = split3(ua)
    mh, mm, ml = split3(um)
    left = jnp.concatenate([a, a, b, a, c, b], 0)
    dn = (((0,), (0,)), ((), ()))
    for lo, (h, m, l) in ((0, (ah, am, al)), (NB, (mh, mm, ml))):
        right = jnp.concatenate([h, m, h, l, h, m], 0)
        W[:, lo:lo + NB] = W[:, lo:lo + NB] - lax.dot_general(left, right, dn, preferred_element_type=F32)


def kernel(m_ref, o_ref, a_ref, x0, x1, D, E, W, via, asem, zsend, zrecv, vsend, vrecv, gsend, grecv, bsend, brecv, ssend, srecv, esend, erecv):
    row = lax.axis_index("row")
    z = lax.axis_index("col")
    core = lax.rem(row, 2)
    x = lax.rem(row // 2, XS)
    y = row // (2 * XS)

    def at(x_, y_, z_, c_):
        return ((y_ * XS + x_) * 2 + c_, z_)

    is_src = (row == 0) & (z == 0)
    is_a11 = (row == 1) & (z == 1)
    is_a10 = (row == 1) & (z == 0)

    barrier = pltpu.get_barrier_semaphore()
    for d in range(1, ZS):
        pl.semaphore_signal(barrier, inc=1, device_id=at(x, y, lax.rem(z + d, ZS), core), device_id_type=MESH)
    for d in range(1, YS):
        pl.semaphore_signal(barrier, inc=1, device_id=at(x, lax.rem(y + d, YS), z, core), device_id_type=MESH)
    for d in range(1, XS):
        pl.semaphore_signal(barrier, inc=1, device_id=at(lax.rem(x + d, XS), y, z, core), device_id_type=MESH)
    pl.semaphore_signal(barrier, inc=1, device_id=at(x, y, z, 1 - core), device_id_type=MESH)

    for d in (1, ZS - 1):
        pl.semaphore_signal(barrier, inc=1, device_id=at(x, y, lax.rem(z + d, ZS), 1 - core), device_id_type=MESH)

    @pl.when(is_src)
    def _():
        pl.semaphore_signal(barrier, inc=1, device_id=(1, 1), device_id_type=MESH)

    @pl.when(is_a11)
    def _():
        pl.semaphore_signal(barrier, inc=1, device_id=(0, 0), device_id_type=MESH)

    own = pltpu.make_async_copy(m_ref, a_ref, asem)
    own.start()

    @pl.when(z < 2)
    def _():
        own.wait()

    @pl.when(z == 0)
    def _():
        for s in range(4):
            x0[s] = a_ref[s].astype(F32)

        @pl.when(row == 0)
        def _():
            x0[0] = symmetric(x0[0])

    @pl.when(z == 1)
    def _():
        for s in range(4):
            x1[s] = a_ref[s].astype(F32)

        @pl.when(row == 1)
        def _():
            x1[0] = symmetric(x1[0])

    @pl.when(is_src)
    def _():
        factor_start(W, x0[0])

        def step(k, carry):
            factor_step(W, k)
            return carry

        lax.fori_loop(0, EARLY, step, 0)

    pl.semaphore_wait(barrier, ZS + YS + XS + jnp.where(is_src | is_a11, 1, 0))

    def send_a10():
        return pltpu.make_async_remote_copy(src_ref=x0.at[0], dst_ref=E.at[0], send_sem=esend.at[0], recv_sem=erecv.at[0],
                                            device_id=(0, 0), device_id_type=MESH)

    def send_a11():
        return pltpu.make_async_remote_copy(src_ref=x1.at[0], dst_ref=E.at[1], send_sem=esend.at[0], recv_sem=erecv.at[1],
                                            device_id=(0, 0), device_id_type=MESH)

    @pl.when(is_a10)
    def _():
        send_a10().start()

    @pl.when(is_a11)
    def _():
        send_a11().start()

    goal = 2 * x + core

    def hand(p, q):
        rows = pl.ds(q * PIECE, PIECE)
        return pltpu.make_async_remote_copy(src_ref=(x0, x1)[p].at[0, rows, :], dst_ref=D.at[AJ0 + p, rows, :],
                                            send_sem=bsend.at[AJ0 + p, q], recv_sem=brecv.at[AJ0 + p, q],
                                            device_id=at(x, q, z, core), device_id_type=MESH)

    def hand_first(p):
        rows = pl.ds(0, PIECE)
        return pltpu.make_async_remote_copy(src_ref=(x0, x1)[p].at[0, rows, :], dst_ref=D.at[AJ0 + p, rows, :],
                                            send_sem=bsend.at[AJ0 + p, 0], recv_sem=brecv.at[AJ0 + p, 0],
                                            device_id=at(x, y, goal, core), device_id_type=MESH)

    def hand_on(p):
        ref = D.at[AJ0 + p, pl.ds(pl.multiple_of(y * PIECE, PIECE), PIECE), :]
        return pltpu.make_async_remote_copy(src_ref=ref, dst_ref=ref, send_sem=bsend.at[AJ0 + p, 0], recv_sem=brecv.at[AJ0 + p, y],
                                            device_id=at(x, y, goal, core), device_id_type=MESH)

    def hand_out(act):
        for p in range(2):
            @pl.when((z == p) & (goal >= 2) & (y == 0))
            def _():
                act(hand_first(p))
                for q in range(1, YS):
                    act(hand(p, q))

    def hand_over(act):
        for p in range(2):
            @pl.when((z == p) & (goal >= 2) & (y > 0))
            def _():
                act(p)

    def pass_on(p):
        hand_on(p).wait_recv()
        hand_on(p).start()

    hand_out(lambda cp: cp.start())

    hops = z, lax.rem(ZS - z, ZS), lax.rem(z + ZS - 1, ZS), lax.rem(ZS + 1 - z, ZS), z
    up, down = lax.rem(z + 1, ZS), lax.rem(z + ZS - 1, ZS)
    other = at(x, y, z, 1 - core)

    def place(st, c):
        buf = x0 if st < 2 or st == 4 else x1
        odd = 0 if st in (0, 2) else 1
        u = jnp.where(c < RING, 2 * c + odd, c + RING)
        per = NB // R
        return buf.at[u // per, pl.ds(pl.multiple_of(lax.rem(u, per) * R, R), R), :]

    def to(st, core_):
        return at(x, y, down if st in (1, 3) else up, core_)

    def zcopy(st, c):
        ref = place(st, c)
        return pltpu.make_async_remote_copy(src_ref=ref, dst_ref=ref, send_sem=zsend.at[st, c], recv_sem=zrecv.at[st, c],
                                            device_id=to(st, core), device_id_type=MESH)

    def enter(st, c):
        return pltpu.make_async_remote_copy(src_ref=place(st, c), dst_ref=via.at[st // 2, c], send_sem=zsend.at[st, c],
                                            recv_sem=vrecv.at[st // 2, c], device_id=to(st, 1 - core), device_id_type=MESH)

    def vcopy(st, c):
        ref = via.at[st // 2, c]
        return pltpu.make_async_remote_copy(src_ref=ref, dst_ref=ref, send_sem=vsend.at[st // 2, c], recv_sem=vrecv.at[st // 2, c],
                                            device_id=to(st, core), device_id_type=MESH)

    def give(st, c):
        return pltpu.make_async_remote_copy(src_ref=via.at[st // 2, c], dst_ref=place(st, c), send_sem=gsend.at[st // 2, c],
                                            recv_sem=grecv.at[st // 2, c], device_id=other, device_id_type=MESH)

    def takes(st, c):
        if st == 0:
            return (z >= 1) & ((c < RING) | (z <= MID))
        if st == 1:
            return (z >= 2) & ((c < RING) | (z > MID))
        if st == 2:
            return (z >= 2) & ((c < RING) | (z <= MID))
        if st == 3:
            return (z != 1) & ((c < RING) | (z == 0) | (z > MID))
        return (z == 1) & (c < RING)

    def passes(st, c):
        if st == 0:
            return (z < ZS - 1) & ((c < RING) | (z < MID))
        if st == 1:
            return (z != 1) & (z != 2) & ((c < RING) | (z == 0) | (z > MID + 1))
        if st == 2:
            return (z >= 1) & (z < ZS - 1) & ((c < RING) | (z < MID))
        if st == 3:
            return (z != 2) & ((c < RING) | (z < 2) | (z > MID + 1))
        return (z == 0) & (c < RING)

    def on_lane(st):
        return core == st % 2

    def begins(st):
        return z == st // 2

    def keeps(st):
        return z != 0

    def ztick(n):
        for st in range(4):
            c = n - (hops[st] * SKEW) // 4
            ok = (c >= 0) & (c < COUNT)

            @pl.when(ok & on_lane(st))
            def _():
                @pl.when(takes(st, c))
                def _():
                    zcopy(st, c).wait_recv()

                @pl.when(passes(st, c))
                def _():
                    zcopy(st, c).start()

                @pl.when(takes(st, c))
                def _():
                    vcopy(st, c).wait_recv()

                    @pl.when(passes(st, c))
                    def _():
                        vcopy(st, c).start()

                    @pl.when(keeps(st))
                    def _():
                        give(st, c).start()

            @pl.when(ok & jnp.logical_not(on_lane(st)) & begins(st))
            def _():
                enter(st, c).start()

        c = n - (hops[4] * SKEW) // 4

        @pl.when((c >= 0) & (c < COUNT) & passes(4, c))
        def _():
            zcopy(4, c).start()

    def zfinish(c, carry):
        @pl.when(takes(4, c))
        def _():
            zcopy(4, c).wait_recv()

        for st in range(4):
            @pl.when(jnp.logical_not(on_lane(st)) & takes(st, c) & keeps(st))
            def _():
                give(st, c).wait_recv()
        return carry

    def root(b):
        if b < AJ0:
            return 0, 0, 0
        return z // 2, z, lax.rem(z, 2)

    def has(b):
        return z >= (0 if b == INV0 else 1 if b < AJ0 else 2)

    def piece(b, q, dest, sem):
        ref = D.at[b, pl.ds(pl.multiple_of(q * PIECE, PIECE), PIECE), :]
        return pltpu.make_async_remote_copy(src_ref=ref, dst_ref=ref, send_sem=bsend.at[b, sem], recv_sem=brecv.at[b, q],
                                            device_id=dest, device_id_type=MESH)

    def on_root(b):
        xr, zr, cr = root(b)
        return (x == xr) & (y == 0) & (z == zr) & (core == cr) & (b < AJ0)

    def scatter(b, act):
        for d in range(1, YS):
            act(piece(b, d, at(x, d, z, core), d - 1))

    def send_x(b, act):
        for d in range(1, XS):
            act(piece(b, y, at(lax.rem(x + d, XS), y, z, core), 7 + d))

    def send_z(b, act):
        for d in range(1, ZS):
            act(piece(b, y, at(x, y, d, core), 10 + d))

    def send_y(b, act):
        xr, zr, _ = root(b)
        for d in range(1, YS):
            to = lax.rem(y + d, YS)

            @pl.when(jnp.logical_not((to == 0) & (x == xr) & (z == zr) & (b < AJ0)))
            def _():
                act(piece(b, y, at(x, to, z, core), 17 + d))

    def start(cp):
        cp.start()

    def finish(cp):
        cp.wait_send()

    def relay_sends(b, act):
        xr, zr, cr = root(b)
        on_core = core == cr

        @pl.when(on_core & (x == xr) & (z == zr) & (z >= (2 if b >= AJ0 else 0)))
        def _():
            send_x(b, act)

        if b < AJ0:
            @pl.when(on_core & (z == zr))
            def _():
                send_z(b, act)

        @pl.when(on_core & has(b))
        def _():
            send_y(b, act)

    def relay(b):
        xr, zr, cr = root(b)
        gets = (core == cr) & ((has(b) | (z == zr)) if b < AJ0 else has(b))

        @pl.when(gets & jnp.logical_not(on_root(b)))
        def _():
            piece(b, y, at(x, y, z, 1 - core), 0).wait_recv()
            relay_sends(b, start)

    def sibling(b):
        return pltpu.make_async_remote_copy(src_ref=D.at[b], dst_ref=D.at[b], send_sem=ssend.at[b], recv_sem=srecv.at[b],
                                            device_id=at(x, y, z, 1 - core), device_id_type=MESH)

    def collect(b):
        cr = root(b)[2]

        @pl.when((core == cr) & has(b))
        def _():
            @pl.when(jnp.logical_not(on_root(b)))
            def _():
                for d in range(1, YS):
                    piece(b, lax.rem(y + d, YS), at(x, y, z, 1 - core), 0).wait_recv()
            sibling(b).start()

        @pl.when((core != cr) & has(b))
        def _():
            sibling(b).wait_recv()

    def drain(b):
        cr = root(b)[2]

        @pl.when(on_root(b))
        def _():
            scatter(b, finish)

        relay_sends(b, finish)

        @pl.when((core == cr) & has(b))
        def _():
            sibling(b).wait_send()

    def stream(b, k):
        rows = pl.ds(pl.multiple_of(k * PIECE, PIECE), PIECE)
        D[b, rows, :] = W[rows, NB:2 * NB]

        @pl.when(k > 0)
        def _():
            piece(b, k, at(x, k, z, core), k - 1).start()

        @pl.when(k == 0)
        def _():
            relay_sends(b, start)

    def factor_tick(n):
        k = n + EARLY
        at_p10 = NB // STEP

        @pl.when(is_src & (k < at_p10))
        def _():
            factor_step(W, k)
            stream(INV0, k)

        @pl.when(is_src & (k == at_p10))
        def _():
            send_a10().wait_recv()
            send_a11().wait_recv()
            p10 = mm_nt(E[0], D[INV0])
            D[P10] = p10
            scatter(P10, start)
            relay_sends(P10, start)
            factor_start(W, E[1] - mm_nt(p10, p10))

        @pl.when(is_src & (k > at_p10) & (k <= at_p10 + NB // STEP))
        def _():
            factor_step(W, k - at_p10 - 1)
            stream(INV1, k - at_p10 - 1)

    @pl.when(is_src)
    def _():
        def early(k, carry):
            stream(INV0, k)
            return carry

        lax.fori_loop(0, EARLY, early, 0)

    order = (INV0, P10, AJ0, AJ1, INV1)

    def relay_at(b):
        xr, zr, _ = root(b)
        t = {INV0: AT_INV0 + jnp.maximum(y + 1 - EARLY, 0), P10: AT_P10, INV1: AT_INV1 + y, AJ0: AT_AJ, AJ1: AT_AJ}[b]
        return t + jnp.where(x == xr, 0, TO_X) + (jnp.where(z == zr, 0, TO_Z) if b < AJ0 else 0)

    when = [relay_at(b) for b in order]

    def tick(n, carry):
        ztick(n)
        factor_tick(n)

        @pl.when(n == AT_HAND)
        def _():
            hand_over(pass_on)

        for b, t in zip(order, when):
            @pl.when(n == t)
            def _():
                relay(b)
        return carry

    lax.fori_loop(0, TICKS, tick, 0)
    lax.fori_loop(0, COUNT, zfinish, 0)

    for b in order:
        collect(b)

    @pl.when(z >= 2)
    def _():
        own.wait()

    @pl.when(z == 0)
    def _():
        E[0] = D[INV0]
        E[1] = jnp.zeros((NB, NB), F32)

    @pl.when(z >= 1)
    def _():
        inv0, p10, inv1 = D[INV0], D[P10], D[INV1]

        @pl.when(z == 1)
        def _():
            E[1] = inv1
            E[0] = mm_nn(-mm_nn(inv1, p10), inv0)

        @pl.when(z >= 2)
        def _():
            pj0 = mm_nt(D[AJ0], inv0)
            pj1 = mm_nt(D[AJ1] - mm_nt(pj0, p10), inv1)
            t1 = -mm_nn(pj1, inv1)
            E[1] = t1
            E[0] = -mm_nn(pj0 + mm_nn(t1, p10), inv0)

    dn = (((1,), (1,)), ((), ()))
    t0 = split3(E[0])[::-1]
    t1 = split3(E[1])[::-1]
    for s in range(4):
        acc = jnp.where(z >= 2, a_ref[s].astype(F32), 0.0)
        xs = x0[s].astype(jnp.bfloat16)
        for t in t0:
            acc = acc + lax.dot_general(xs, t, dn, preferred_element_type=F32)
        xs = jnp.where(z >= 1, x1[s], 0.0).astype(jnp.bfloat16)
        for t in t1:
            acc = acc + lax.dot_general(xs, t, dn, preferred_element_type=F32)
        if s == 0:
            acc = jnp.where((row > z) | (row * NB + iota((NB, NB), 0) >= z * NB + iota((NB, NB), 1)), acc, 0.0)
        for h in range(2):
            o_ref[pl.ds(2 * NB * s + h, NB, stride=2), :] = acc[:, 128 * h:128 * h + 128]

    @pl.when(is_a10)
    def _():
        send_a10().wait_send()

    @pl.when(is_a11)
    def _():
        send_a11().wait_send()

    def zdrain(c, carry):
        for st in range(4):
            @pl.when(on_lane(st) & passes(st, c))
            def _():
                zcopy(st, c).wait_send()

            @pl.when(on_lane(st) & takes(st, c))
            def _():
                @pl.when(passes(st, c))
                def _():
                    vcopy(st, c).wait_send()

                @pl.when(keeps(st))
                def _():
                    give(st, c).wait_send()

            @pl.when(jnp.logical_not(on_lane(st)) & begins(st))
            def _():
                enter(st, c).wait_send()

        @pl.when(passes(4, c))
        def _():
            zcopy(4, c).wait_send()
        return carry

    lax.fori_loop(0, COUNT, zdrain, 0)

    hand_out(finish)
    hand_over(lambda p: hand_on(p).wait_send())
    for b in order:
        drain(b)


def per_device(matrix):
    a = matrix.reshape(4, NB, NB)
    dma = pltpu.SemaphoreType.DMA
    out = pl.pallas_call(
        kernel,
        out_shape=jax.ShapeDtypeStruct((8 * NB, 128), F32),
        in_specs=[pl.BlockSpec(memory_space=pltpu.HBM)],
        out_specs=pl.BlockSpec(memory_space=pltpu.VMEM),
        scratch_shapes=[
            pltpu.VMEM((4, NB, NB), jnp.bfloat16),
            pltpu.VMEM((4, NB, NB), F32),
            pltpu.VMEM((4, NB, NB), F32),
            pltpu.VMEM((5, NB, NB), F32),
            pltpu.VMEM((2, NB, NB), F32),
            pltpu.VMEM((NB, 2 * NB), F32),
            pltpu.VMEM((2, COUNT, R, NB), F32),
            dma(()), dma((5, COUNT)), dma((5, COUNT)),
            dma((2, COUNT)), dma((2, COUNT)), dma((2, COUNT)), dma((2, COUNT)),
            dma((5, 25)), dma((5, YS)),
            dma((5,)), dma((5,)),
            dma((1,)), dma((2,)),
        ],
        compiler_params=pltpu.CompilerParams(collective_id=0, has_side_effects=True, vmem_limit_bytes=40 << 20),
    )(a)
    return out.reshape(4, NB, 1, NB)


def solution(mesh):
    return jax.shard_map(
        per_device,
        mesh=mesh,
        in_specs=(P(None, "row", None, "col"),),
        out_specs=P(None, "row", None, "col"),
        check_vma=False,
    )
```

```python
import jax
import jax.numpy as jnp
from jax import lax
from jax.experimental import pallas as pl
from jax.experimental.pallas import tpu as pltpu
from jax.sharding import PartitionSpec as P

MESH = pl.DeviceIdType.MESH
F32 = jnp.float32
NB = 256
STEP = 32
XS, YS, ZS = 4, 8, 8
R = 32
SKEW = 12
UNITS = 4 * NB // R
RING = 13
COUNT = UNITS - RING
EARLY = 4
MID = 4
TICKS = 40
PIECE = NB // YS
INV0, P10, INV1, AJ0, AJ1 = range(5)
AT_INV0, AT_P10, AT_INV1, AT_AJ, AT_HAND = 3, 9, 11, 9, 4
TO_X, TO_Z = 3, 4


def split3(x):
    h = x.astype(jnp.bfloat16)
    r = x - h.astype(F32)
    m = r.astype(jnp.bfloat16)
    return h, m, (r - m.astype(F32)).astype(jnp.bfloat16)


def mm_nt(a, b):
    return lax.dot_general(a, b, (((1,), (1,)), ((), ())), precision=lax.Precision.HIGHEST, preferred_element_type=F32)


def mm_nn(a, b):
    return lax.dot_general(a, b, (((1,), (0,)), ((), ())), precision=lax.Precision.HIGHEST, preferred_element_type=F32)


def iota(shape, d):
    return lax.broadcasted_iota(jnp.int32, shape, d)


def symmetric(x):
    keep = iota((NB, NB), 0) >= iota((NB, NB), 1)
    return jnp.where(keep, x, x.T)


def factor_start(W, a):
    W[:, 0:NB] = a
    W[:, NB:2 * NB] = jnp.where(iota((NB, NB), 0) == iota((NB, NB), 1), 1.0, 0.0).astype(F32)


def factor_step(W, k):
    base = pl.multiple_of(STEP * k, STEP)
    ra = W[pl.ds(base, STEP), 0:NB]
    rm = W[pl.ds(base, STEP), NB:2 * NB]
    ra = pltpu.roll(ra, lax.rem(NB - STEP * k, NB), 1)
    G = [[ra[8 * g:8 * g + 8, 0:128], ra[8 * g:8 * g + 8, 128:256],
          rm[8 * g:8 * g + 8, 0:128], rm[8 * g:8 * g + 8, 128:256]] for g in range(4)]
    full = (8, 128)
    sub = iota(full, 0)
    for t in range(4):
        cols = {g: [jnp.broadcast_to(G[g][0][:, 8 * t + i:8 * t + i + 1], full) for i in range(8)] for g in range(t, 4)}
        s = {(i, j): jnp.broadcast_to(cols[t][j][i:i + 1, :], full) for j in range(8) for i in range(j, 8)}
        row = [[jnp.broadcast_to(G[t][v][i:i + 1, :], full) for v in range(4)] for i in range(8)]
        for j in range(8):
            r = lax.rsqrt(s[j, j])
            for i in range(j + 1, 8):
                s[i, j] = s[i, j] * r
            for i2 in range(j + 1, 8):
                for i in range(i2, 8):
                    s[i, i2] = s[i, i2] - s[i, j] * s[i2, j]
            row[j] = [x * r for x in row[j]]
            for i in range(j + 1, 8):
                row[i] = [x - s[i, j] * y for x, y in zip(row[i], row[j])]
            for g in range(t + 1, 4):
                cols[g][j] = cols[g][j] * r
                for i in range(j + 1, 8):
                    cols[g][i] = cols[g][i] - s[i, j] * cols[g][j]
        for g in range(t + 1, 4):
            for v in range(4):
                p = [cols[g][j] * row[j][v] for j in range(8)]
                while len(p) > 1:
                    p = [a + b for a, b in zip(p[::2], p[1::2])]
                G[g][v] = G[g][v] - p[0]
        for v in range(4):
            x = row[0][v]
            for i in range(1, 8):
                x = jnp.where(sub == i, row[i][v], x)
            G[t][v] = x
    ua = jnp.concatenate([jnp.concatenate([G[g][0], G[g][1]], 1) for g in range(4)], 0)
    um = jnp.concatenate([jnp.concatenate([G[g][2], G[g][3]], 1) for g in range(4)], 0)
    ua = pltpu.roll(ua, STEP * k, 1)
    lhs = jnp.where(iota((STEP, NB), 1) >= STEP * (k + 1), ua, 0.0)
    W[pl.ds(base, STEP), 0:NB] = ua
    W[pl.ds(base, STEP), NB:2 * NB] = um
    a, b, c = split3(lhs)
    ah, am, al = split3(ua)
    mh, mm, ml = split3(um)
    left = jnp.concatenate([a, a, b, a, c, b], 0)
    dn = (((0,), (0,)), ((), ()))
    for lo, (h, m, l) in ((0, (ah, am, al)), (NB, (mh, mm, ml))):
        right = jnp.concatenate([h, m, h, l, h, m], 0)
        W[:, lo:lo + NB] = W[:, lo:lo + NB] - lax.dot_general(left, right, dn, preferred_element_type=F32)


def kernel(m_ref, o_ref, a_ref, x0, x1, D, E, W, via, asem, zsend, zrecv, vsend, vrecv, gsend, grecv, bsend, brecv, ssend, srecv, esend, erecv):
    row = lax.axis_index("row")
    z = lax.axis_index("col")
    core = lax.rem(row, 2)
    x = lax.rem(row // 2, XS)
    y = row // (2 * XS)

    def at(x_, y_, z_, c_):
        return ((y_ * XS + x_) * 2 + c_, z_)

    is_src = (row == 0) & (z == 0)
    is_a11 = (row == 1) & (z == 1)
    is_a10 = (row == 1) & (z == 0)

    barrier = pltpu.get_barrier_semaphore()
    for d in range(1, ZS):
        pl.semaphore_signal(barrier, inc=1, device_id=at(x, y, lax.rem(z + d, ZS), core), device_id_type=MESH)
    for d in range(1, YS):
        pl.semaphore_signal(barrier, inc=1, device_id=at(x, lax.rem(y + d, YS), z, core), device_id_type=MESH)
    for d in range(1, XS):
        pl.semaphore_signal(barrier, inc=1, device_id=at(lax.rem(x + d, XS), y, z, core), device_id_type=MESH)
    pl.semaphore_signal(barrier, inc=1, device_id=at(x, y, z, 1 - core), device_id_type=MESH)

    for d in (1, ZS - 1):
        pl.semaphore_signal(barrier, inc=1, device_id=at(x, y, lax.rem(z + d, ZS), 1 - core), device_id_type=MESH)

    @pl.when(is_src)
    def _():
        pl.semaphore_signal(barrier, inc=1, device_id=(1, 1), device_id_type=MESH)

    @pl.when(is_a11)
    def _():
        pl.semaphore_signal(barrier, inc=1, device_id=(0, 0), device_id_type=MESH)

    own = pltpu.make_async_copy(m_ref, a_ref, asem)
    own.start()

    @pl.when(z < 2)
    def _():
        own.wait()

    @pl.when(z == 0)
    def _():
        for s in range(4):
            x0[s] = a_ref[s].astype(F32)

        @pl.when(row == 0)
        def _():
            x0[0] = symmetric(x0[0])

    @pl.when(z == 1)
    def _():
        for s in range(4):
            x1[s] = a_ref[s].astype(F32)

        @pl.when(row == 1)
        def _():
            x1[0] = symmetric(x1[0])

    @pl.when(is_src)
    def _():
        factor_start(W, x0[0])

        def step(k, carry):
            factor_step(W, k)
            return carry

        lax.fori_loop(0, EARLY, step, 0)

    pl.semaphore_wait(barrier, ZS + YS + XS + jnp.where(is_src | is_a11, 1, 0))

    def send_a10():
        return pltpu.make_async_remote_copy(src_ref=x0.at[0], dst_ref=E.at[0], send_sem=esend.at[0], recv_sem=erecv.at[0],
                                            device_id=(0, 0), device_id_type=MESH)

    def send_a11():
        return pltpu.make_async_remote_copy(src_ref=x1.at[0], dst_ref=E.at[1], send_sem=esend.at[0], recv_sem=erecv.at[1],
                                            device_id=(0, 0), device_id_type=MESH)

    @pl.when(is_a10)
    def _():
        send_a10().start()

    @pl.when(is_a11)
    def _():
        send_a11().start()

    goal = 2 * x + core

    def hand(p, q):
        rows = pl.ds(q * PIECE, PIECE)
        return pltpu.make_async_remote_copy(src_ref=(x0, x1)[p].at[0, rows, :], dst_ref=D.at[AJ0 + p, rows, :],
                                            send_sem=bsend.at[AJ0 + p, q], recv_sem=brecv.at[AJ0 + p, q],
                                            device_id=at(x, q, z, core), device_id_type=MESH)

    def hand_first(p):
        rows = pl.ds(0, PIECE)
        return pltpu.make_async_remote_copy(src_ref=(x0, x1)[p].at[0, rows, :], dst_ref=D.at[AJ0 + p, rows, :],
                                            send_sem=bsend.at[AJ0 + p, 0], recv_sem=brecv.at[AJ0 + p, 0],
                                            device_id=at(x, y, goal, core), device_id_type=MESH)

    def hand_on(p):
        ref = D.at[AJ0 + p, pl.ds(pl.multiple_of(y * PIECE, PIECE), PIECE), :]
        return pltpu.make_async_remote_copy(src_ref=ref, dst_ref=ref, send_sem=bsend.at[AJ0 + p, 0], recv_sem=brecv.at[AJ0 + p, y],
                                            device_id=at(x, y, goal, core), device_id_type=MESH)

    def hand_out(act):
        for p in range(2):
            @pl.when((z == p) & (goal >= 2) & (y == 0))
            def _():
                act(hand_first(p))
                for q in range(1, YS):
                    act(hand(p, q))

    def hand_over(act):
        for p in range(2):
            @pl.when((z == p) & (goal >= 2) & (y > 0))
            def _():
                act(p)

    def pass_on(p):
        hand_on(p).wait_recv()
        hand_on(p).start()

    hand_out(lambda cp: cp.start())

    hops = z, lax.rem(ZS - z, ZS), lax.rem(z + ZS - 1, ZS), lax.rem(ZS + 1 - z, ZS), z
    up, down = lax.rem(z + 1, ZS), lax.rem(z + ZS - 1, ZS)
    other = at(x, y, z, 1 - core)

    def place(st, c):
        buf = x0 if st < 2 or st == 4 else x1
        odd = 0 if st in (0, 2) else 1
        u = jnp.where(c < RING, 2 * c + odd, c + RING)
        per = NB // R
        return buf.at[u // per, pl.ds(pl.multiple_of(lax.rem(u, per) * R, R), R), :]

    def to(st, core_):
        return at(x, y, down if st in (1, 3) else up, core_)

    def zcopy(st, c):
        ref = place(st, c)
        return pltpu.make_async_remote_copy(src_ref=ref, dst_ref=ref, send_sem=zsend.at[st, c], recv_sem=zrecv.at[st, c],
                                            device_id=to(st, core), device_id_type=MESH)

    def enter(st, c):
        return pltpu.make_async_remote_copy(src_ref=place(st, c), dst_ref=via.at[st // 2, c], send_sem=zsend.at[st, c],
                                            recv_sem=vrecv.at[st // 2, c], device_id=to(st, 1 - core), device_id_type=MESH)

    def vcopy(st, c):
        ref = via.at[st // 2, c]
        return pltpu.make_async_remote_copy(src_ref=ref, dst_ref=ref, send_sem=vsend.at[st // 2, c], recv_sem=vrecv.at[st // 2, c],
                                            device_id=to(st, core), device_id_type=MESH)

    def give(st, c):
        return pltpu.make_async_remote_copy(src_ref=via.at[st // 2, c], dst_ref=place(st, c), send_sem=gsend.at[st // 2, c],
                                            recv_sem=grecv.at[st // 2, c], device_id=other, device_id_type=MESH)

    def takes(st, c):
        if st == 0:
            return (z >= 1) & ((c < RING) | (z <= MID))
        if st == 1:
            return (z >= 2) & ((c < RING) | (z > MID))
        if st == 2:
            return (z >= 2) & ((c < RING) | (z <= MID))
        if st == 3:
            return (z != 1) & ((c < RING) | (z == 0) | (z > MID))
        return (z == 1) & (c < RING)

    def passes(st, c):
        if st == 0:
            return (z < ZS - 1) & ((c < RING) | (z < MID))
        if st == 1:
            return (z != 1) & (z != 2) & ((c < RING) | (z == 0) | (z > MID + 1))
        if st == 2:
            return (z >= 1) & (z < ZS - 1) & ((c < RING) | (z < MID))
        if st == 3:
            return (z != 2) & ((c < RING) | (z < 2) | (z > MID + 1))
        return (z == 0) & (c < RING)

    def on_lane(st):
        return core == st % 2

    def begins(st):
        return z == st // 2

    def keeps(st):
        return z != 0

    def ztick(n):
        for st in range(4):
            c = n - (hops[st] * SKEW) // 4
            ok = (c >= 0) & (c < COUNT)

            @pl.when(ok & on_lane(st))
            def _():
                @pl.when(takes(st, c))
                def _():
                    zcopy(st, c).wait_recv()

                @pl.when(passes(st, c))
                def _():
                    zcopy(st, c).start()

                @pl.when(takes(st, c))
                def _():
                    vcopy(st, c).wait_recv()

                    @pl.when(passes(st, c))
                    def _():
                        vcopy(st, c).start()

                    @pl.when(keeps(st))
                    def _():
                        give(st, c).start()

            @pl.when(ok & jnp.logical_not(on_lane(st)) & begins(st))
            def _():
                enter(st, c).start()

        c = n - COUNT

        @pl.when((c >= 0) & (c < COUNT) & passes(4, c))
        def _():
            zcopy(4, c).start()

    def zfinish(c, carry):
        @pl.when(takes(4, c))
        def _():
            zcopy(4, c).wait_recv()

        for st in range(4):
            @pl.when(jnp.logical_not(on_lane(st)) & takes(st, c) & keeps(st))
            def _():
                give(st, c).wait_recv()
        return carry

    def root(b):
        if b < AJ0:
            return 0, 0, 0
        return z // 2, z, lax.rem(z, 2)

    def has(b):
        return z >= (0 if b == INV0 else 1 if b < AJ0 else 2)

    def piece(b, q, dest, sem):
        ref = D.at[b, pl.ds(pl.multiple_of(q * PIECE, PIECE), PIECE), :]
        return pltpu.make_async_remote_copy(src_ref=ref, dst_ref=ref, send_sem=bsend.at[b, sem], recv_sem=brecv.at[b, q],
                                            device_id=dest, device_id_type=MESH)

    def on_root(b):
        xr, zr, cr = root(b)
        return (x == xr) & (y == 0) & (z == zr) & (core == cr) & (b < AJ0)

    def scatter(b, act):
        for d in range(1, YS):
            act(piece(b, d, at(x, d, z, core), d - 1))

    def send_x(b, act):
        for d in range(1, XS):
            act(piece(b, y, at(lax.rem(x + d, XS), y, z, core), 7 + d))

    def send_z(b, act):
        for d in range(1, ZS):
            act(piece(b, y, at(x, y, d, core), 10 + d))

    def send_y(b, act):
        xr, zr, _ = root(b)
        for d in range(1, YS):
            to = lax.rem(y + d, YS)

            @pl.when(jnp.logical_not((to == 0) & (x == xr) & (z == zr) & (b < AJ0)))
            def _():
                act(piece(b, y, at(x, to, z, core), 17 + d))

    def start(cp):
        cp.start()

    def finish(cp):
        cp.wait_send()

    def relay_sends(b, act):
        xr, zr, cr = root(b)
        on_core = core == cr

        @pl.when(on_core & (x == xr) & (z == zr) & (z >= (2 if b >= AJ0 else 0)))
        def _():
            send_x(b, act)

        if b < AJ0:
            @pl.when(on_core & (z == zr))
            def _():
                send_z(b, act)

        @pl.when(on_core & has(b))
        def _():
            send_y(b, act)

    def relay(b):
        xr, zr, cr = root(b)
        gets = (core == cr) & ((has(b) | (z == zr)) if b < AJ0 else has(b))

        @pl.when(gets & jnp.logical_not(on_root(b)))
        def _():
            piece(b, y, at(x, y, z, 1 - core), 0).wait_recv()
            relay_sends(b, start)

    def sibling(b):
        return pltpu.make_async_remote_copy(src_ref=D.at[b], dst_ref=D.at[b], send_sem=ssend.at[b], recv_sem=srecv.at[b],
                                            device_id=at(x, y, z, 1 - core), device_id_type=MESH)

    def collect(b):
        cr = root(b)[2]

        @pl.when((core == cr) & has(b))
        def _():
            @pl.when(jnp.logical_not(on_root(b)))
            def _():
                for d in range(1, YS):
                    piece(b, lax.rem(y + d, YS), at(x, y, z, 1 - core), 0).wait_recv()
            sibling(b).start()

        @pl.when((core != cr) & has(b))
        def _():
            sibling(b).wait_recv()

    def drain(b):
        cr = root(b)[2]

        @pl.when(on_root(b))
        def _():
            scatter(b, finish)

        relay_sends(b, finish)

        @pl.when((core == cr) & has(b))
        def _():
            sibling(b).wait_send()

    def stream(b, k):
        rows = pl.ds(pl.multiple_of(k * PIECE, PIECE), PIECE)
        D[b, rows, :] = W[rows, NB:2 * NB]

        @pl.when(k > 0)
        def _():
            piece(b, k, at(x, k, z, core), k - 1).start()

        @pl.when(k == 0)
        def _():
            relay_sends(b, start)

    def factor_tick(n):
        k = n + EARLY
        at_p10 = NB // STEP

        @pl.when(is_src & (k < at_p10))
        def _():
            factor_step(W, k)
            stream(INV0, k)

        @pl.when(is_src & (k == at_p10))
        def _():
            send_a10().wait_recv()
            send_a11().wait_recv()
            p10 = mm_nt(E[0], D[INV0])
            D[P10] = p10
            scatter(P10, start)
            relay_sends(P10, start)
            factor_start(W, E[1] - mm_nt(p10, p10))

        @pl.when(is_src & (k > at_p10) & (k <= at_p10 + NB // STEP))
        def _():
            factor_step(W, k - at_p10 - 1)
            stream(INV1, k - at_p10 - 1)

    @pl.when(is_src)
    def _():
        def early(k, carry):
            stream(INV0, k)
            return carry

        lax.fori_loop(0, EARLY, early, 0)

    order = (INV0, P10, AJ0, AJ1, INV1)

    def relay_at(b):
        xr, zr, _ = root(b)
        t = {INV0: AT_INV0 + jnp.maximum(y + 1 - EARLY, 0), P10: AT_P10, INV1: AT_INV1 + y, AJ0: AT_AJ, AJ1: AT_AJ}[b]
        return t + jnp.where(x == xr, 0, TO_X) + (jnp.where(z == zr, 0, TO_Z) if b < AJ0 else 0)

    when = [relay_at(b) for b in order]

    def tick(n, carry):
        ztick(n)
        factor_tick(n)

        @pl.when(n == AT_HAND)
        def _():
            hand_over(pass_on)

        for b, t in zip(order, when):
            @pl.when(n == t)
            def _():
                relay(b)
        return carry

    lax.fori_loop(0, TICKS, tick, 0)
    lax.fori_loop(0, COUNT, zfinish, 0)

    for b in order:
        collect(b)

    @pl.when(z >= 2)
    def _():
        own.wait()

    @pl.when(z == 0)
    def _():
        E[0] = D[INV0]
        E[1] = jnp.zeros((NB, NB), F32)

    @pl.when(z >= 1)
    def _():
        inv0, p10, inv1 = D[INV0], D[P10], D[INV1]

        @pl.when(z == 1)
        def _():
            E[1] = inv1
            E[0] = mm_nn(-mm_nn(inv1, p10), inv0)

        @pl.when(z >= 2)
        def _():
            pj0 = mm_nt(D[AJ0], inv0)
            pj1 = mm_nt(D[AJ1] - mm_nt(pj0, p10), inv1)
            t1 = -mm_nn(pj1, inv1)
            E[1] = t1
            E[0] = -mm_nn(pj0 + mm_nn(t1, p10), inv0)

    dn = (((1,), (1,)), ((), ()))
    t0 = split3(E[0])[::-1]
    t1 = split3(E[1])[::-1]
    for s in range(4):
        acc = jnp.where(z >= 2, a_ref[s].astype(F32), 0.0)
        xs = x0[s].astype(jnp.bfloat16)
        for t in t0:
            acc = acc + lax.dot_general(xs, t, dn, preferred_element_type=F32)
        xs = jnp.where(z >= 1, x1[s], 0.0).astype(jnp.bfloat16)
        for t in t1:
            acc = acc + lax.dot_general(xs, t, dn, preferred_element_type=F32)
        if s == 0:
            acc = jnp.where((row > z) | (row * NB + iota((NB, NB), 0) >= z * NB + iota((NB, NB), 1)), acc, 0.0)
        for h in range(2):
            o_ref[pl.ds(2 * NB * s + h, NB, stride=2), :] = acc[:, 128 * h:128 * h + 128]

    @pl.when(is_a10)
    def _():
        send_a10().wait_send()

    @pl.when(is_a11)
    def _():
        send_a11().wait_send()

    def zdrain(c, carry):
        for st in range(4):
            @pl.when(on_lane(st) & passes(st, c))
            def _():
                zcopy(st, c).wait_send()

            @pl.when(on_lane(st) & takes(st, c))
            def _():
                @pl.when(passes(st, c))
                def _():
                    vcopy(st, c).wait_send()

                @pl.when(keeps(st))
                def _():
                    give(st, c).wait_send()

            @pl.when(jnp.logical_not(on_lane(st)) & begins(st))
            def _():
                enter(st, c).wait_send()

        @pl.when(passes(4, c))
        def _():
            zcopy(4, c).wait_send()
        return carry

    lax.fori_loop(0, COUNT, zdrain, 0)

    hand_out(finish)
    hand_over(lambda p: hand_on(p).wait_send())
    for b in order:
        drain(b)


def per_device(matrix):
    a = matrix.reshape(4, NB, NB)
    dma = pltpu.SemaphoreType.DMA
    out = pl.pallas_call(
        kernel,
        out_shape=jax.ShapeDtypeStruct((8 * NB, 128), F32),
        in_specs=[pl.BlockSpec(memory_space=pltpu.HBM)],
        out_specs=pl.BlockSpec(memory_space=pltpu.VMEM),
        scratch_shapes=[
            pltpu.VMEM((4, NB, NB), jnp.bfloat16),
            pltpu.VMEM((4, NB, NB), F32),
            pltpu.VMEM((4, NB, NB), F32),
            pltpu.VMEM((5, NB, NB), F32),
            pltpu.VMEM((2, NB, NB), F32),
            pltpu.VMEM((NB, 2 * NB), F32),
            pltpu.VMEM((2, COUNT, R, NB), F32),
            dma(()), dma((5, COUNT)), dma((5, COUNT)),
            dma((2, COUNT)), dma((2, COUNT)), dma((2, COUNT)), dma((2, COUNT)),
            dma((5, 25)), dma((5, YS)),
            dma((5,)), dma((5,)),
            dma((1,)), dma((2,)),
        ],
        compiler_params=pltpu.CompilerParams(collective_id=0, has_side_effects=True, vmem_limit_bytes=40 << 20),
    )(a)
    return out.reshape(4, NB, 1, NB)


def solution(mesh):
    return jax.shard_map(
        per_device,
        mesh=mesh,
        in_specs=(P(None, "row", None, "col"),),
        out_specs=P(None, "row", None, "col"),
        check_vma=False,
    )
```
